32 devices in a mesh: particle: 4 (over z), space: 8 (over y, x, core).
Axes of the slice: x: 2, y: 2, z: 4, core: 2. Of those that a mesh axis runs over, the one named last changes fastest.
Arguments:
- stream: float32 [4, 512, 2048], P('particle', 'space'), may hold values from -6 to 6
- depth_field: float32 [512, 2048], P('space'), may hold values from 0.5 to 4
- obs_col: int32 [512, 16], P('space'), may hold values from 0 to 2047
- obs_val: float32 [512, 16], P('space'), may hold values from -6 to 6
- obs_weight: float32 [512, 16], P('space'), may hold values from 0.1 to 1
- log_weight: float32 [4], P('particle'), may hold values from -6144 to 6144
- target: float32 [1], replicated, may hold values from 0 to 2048
- spectrum: float32 [512, 512], P('space'), may hold values from 1 to 10
- noise_coef: bfloat16 [4, 512, 512], P('particle', 'space'), may hold values from -6 to 6
- selection: int32 [2, 4], replicated, may hold values from 0 to 1
Outputs:
- analysis: float32 [4, 512, 2048], P('particle', 'space')
- misfit_out: float32 [4], P('particle')
The draws below stay inside these ranges and needn't reach their ends.
All inputs are finite; a program needn't handle non-finite values.
Results may differ from the reference program's by a relative error of at most 0.0003.
The reference program's roundings to bfloat16 on the way (of `gradient`, `row_modes`, `shaped` and `inverted`) count: a program that leaves them out, or rounds other values in their place, can miss the bound.
Values may be sent and summed in bfloat16 or wider, within the bound.
A program may use at most 64 MiB of HBM per device.

```python
import math
import jax
import jax.numpy as jnp
from jax import lax

NX = 2048
P_DEV = 1
KM = 256
OBS_ROW = 16
ITERS = 2
SECTIONS = 2
NY = 512
PARTICLES = 4
MODES = 512


def plant(values, rng, low, high):
    spot = [jax.random.randint(jax.random.fold_in(rng, axis), (), 0, length) for axis, length in enumerate(values.shape)]
    longest = values.shape.index(max(values.shape))
    next_to = spot[:longest] + [(spot[longest] + 1) % values.shape[longest]] + spot[longest + 1:]
    return values.at[tuple(spot)].set(low).at[tuple(next_to)].set(high)


def steps_of(rng, shape, cuts, least, high):
    level, own = 1.0, jax.random.fold_in(rng, 6)
    for axis_at, blocks in cuts:
        heights = jnp.exp(jax.random.uniform(jax.random.fold_in(own, axis_at), (blocks,), jnp.float32, least / len(cuts), high / len(cuts)))
        level = level * jnp.repeat(heights, shape[axis_at] // blocks).reshape([-1 if axis == axis_at else 1 for axis in range(len(shape))])
    return level


def normal_values(key, dims, spread, bound, cuts=(), held_as=jnp.bfloat16):
    array = jax.random.normal(key, dims, jnp.float32) * spread
    if len(cuts) > 0:
        array = steps_of(key, dims, cuts, -0.22, 0.18) * array
    return jnp.clip(array, min=-bound, max=bound).astype(held_as)


def setup_inputs(seed: int = 0) -> dict:
    key_of = jax.random.split(jax.random.key(seed), 11)
    return {
        "stream": normal_values(key_of[0], (PARTICLES, NY, NX), 1.0, 6.0, ((0, 4), (1, 8)), jnp.float32),
        "depth_field": jnp.clip(jnp.exp(math.log(4.0) - 2.0794415 * jax.random.uniform(key_of[1], (NY, NX), jnp.float32) ** steps_of(key_of[1], (NY, NX), ((0, 8),), -0.2, 0.2)), 0.5, 4.0),
        "obs_col": plant(jax.random.randint(key_of[2], (NY, OBS_ROW), 0, NX), jax.random.fold_in(key_of[2], 1), 0, NX - 1).astype(jnp.int32),
        "obs_val": normal_values(key_of[3], (NY, OBS_ROW), 1.0, 6.0, ((0, 8),), jnp.float32),
        "obs_weight": jnp.clip(jnp.exp(math.log(1.0) - 2.3025851 * jax.random.uniform(key_of[4], (NY, OBS_ROW), jnp.float32) ** steps_of(key_of[4], (NY, OBS_ROW), ((0, 8),), -0.2, 0.2)), 0.1, 1.0),
        "log_weight": normal_values(key_of[5], (PARTICLES,), (OBS_ROW * NY // 8), 6144.0, ((0, 4),), jnp.float32),
        "target": jnp.clip(jax.random.uniform(key_of[6], (1,), jnp.float32, 0.0, 2048.0), 0.0, 2048.0),
        "spectrum": jnp.clip(jnp.exp(math.log(10.0) - 2.3025851 * jax.random.uniform(key_of[7], (MODES, MODES), jnp.float32) ** steps_of(key_of[7], (MODES, MODES), ((0, 8),), -0.2, 0.2)), 1.0, 10.0),
        "noise_coef": normal_values(key_of[8], (PARTICLES, MODES, MODES), 1.0, 6.0, ((0, 4), (1, 8))),
        "selection": plant(jax.random.randint(key_of[9], (SECTIONS, PARTICLES), 0, 2 * P_DEV), jax.random.fold_in(key_of[9], 1), 0, (2 * P_DEV) - 1).astype(jnp.int32),
    }


STRETCH = 0.05
RELAX_RATE = 0.8
NOISE_AMP = 0.3

def tables(extent, half_modes):
    cell_index = jnp.arange(extent, dtype=jnp.int32)[:, None]
    frequency = jnp.arange(half_modes + 1, dtype=jnp.int32)[None, :]
    angles = (cell_index * frequency % extent).astype(jnp.float32) * (2.0 * math.pi / extent)
    cosines = jnp.cos(angles).astype(jnp.bfloat16)
    sines = jnp.sin(angles[:, 1:half_modes]).astype(jnp.bfloat16)
    return jnp.concatenate([cosines, sines], axis=1)

def compare_obs(grid_field, obs_col, obs_val, obs_weight):
    index_grid = jnp.broadcast_to(obs_col, grid_field.shape[:-1] + obs_col.shape[-1:])
    seen_vals = jnp.take_along_axis(grid_field, index_grid, axis=-1)
    mismatch_vals = obs_val - seen_vals
    return (mismatch_vals, 0.5 * lax.optimization_barrier(jnp.sum(obs_weight * mismatch_vals * mismatch_vals, axis=(-2, -1))))

def spread_obs(weighted_miss, obs_col, columns):
    row_index = jnp.broadcast_to(jnp.arange(obs_col.shape[0], dtype=jnp.int32)[:, None], obs_col.shape)
    return jnp.zeros((obs_col.shape[0], columns), jnp.float32).at[row_index, obs_col].add(weighted_miss)

def operate(grid_field, screening):
    padded = jnp.pad(grid_field, ((1, 1), (0, 0)))
    return padded[2:] + padded[:-2] + jnp.roll(grid_field, 1, axis=1) + jnp.roll(grid_field, -1, axis=1) - (4.0 + screening) * grid_field

def reference(stream, depth_field, obs_col, obs_val, obs_weight, log_weight, target, spectrum, noise_coef, selection):
    x_table = tables(NX, KM)
    y_table = tables(NY, KM)
    norm_factor = 4.0 / (NX * NY)
    screening = STRETCH / depth_field

    def one_member(packed):
        grid_field, member_weight, member_noise = packed
        mismatch_vals, misfit = compare_obs(grid_field, obs_col, obs_val, obs_weight)
        gradient = spread_obs(obs_weight * mismatch_vals, obs_col, NX).astype(jnp.bfloat16)
        row_modes = jnp.dot(gradient, x_table, preferred_element_type=jnp.float32).astype(jnp.bfloat16)
        coefficients = jnp.dot(row_modes.T, y_table, preferred_element_type=jnp.float32)
        weighted = coefficients * (norm_factor * spectrum)
        energy = jnp.sum(coefficients * weighted)
        shaped = (jnp.sqrt(norm_factor * spectrum) * member_noise.astype(jnp.float32)).astype(jnp.bfloat16)
        stacked = jnp.stack([weighted.astype(jnp.bfloat16), shaped]).astype(jnp.float32)
        inverted = jnp.einsum('qkm,ym->qky', stacked, y_table.astype(jnp.float32), precision=lax.Precision.HIGHEST).astype(jnp.bfloat16)
        pulled = jnp.einsum('qky,xk->qyx', inverted.astype(jnp.float32), x_table.astype(jnp.float32), precision=lax.Precision.HIGHEST)
        step_size = (misfit + member_weight - target[0]) / (energy + 1.0)
        increment = step_size * pulled[0] + NOISE_AMP * pulled[1]
        relaxed = grid_field + increment
        pv_target = operate(grid_field, screening) + increment
        for sweep_index in range(ITERS):
            relaxed = relaxed + RELAX_RATE * (operate(relaxed, screening) - pv_target) / (4.0 + screening)
        return relaxed
    fields = lax.map(one_member, (stream, log_weight, noise_coef))
    slot_index = jnp.arange(fields.shape[0], dtype=jnp.int32)
    island = slot_index // P_DEV
    for section_bit in range(SECTIONS):
        chosen = selection[section_bit]
        partner = jnp.bitwise_xor(island, 1 << section_bit)
        source = jnp.where(chosen < P_DEV, island * P_DEV + chosen, partner * P_DEV + chosen - P_DEV)
        fields = fields[source]
    final_miss, misfit_out = compare_obs(fields, obs_col, obs_val, obs_weight)
    return (fields, misfit_out)
```

```python
import functools
import math

import jax
import jax.numpy as jnp
import ml_dtypes
import numpy as np
from jax import lax
from jax.experimental import pallas as pl
from jax.experimental.pallas import tpu as pltpu
from jax.sharding import PartitionSpec as P

STRETCH = 0.05
RELAX_RATE = 0.8
NOISE_AMP = 0.3
HALO = 8
PIECES = 4
MESH = pl.DeviceIdType.MESH


def tables(extent, half_modes):
    cell_index = np.arange(extent, dtype=np.int32)[:, None]
    frequency = np.arange(half_modes + 1, dtype=np.int32)[None, :]
    angles = (cell_index * frequency % extent).astype(np.float32) * np.float32(2.0 * math.pi / extent)
    cosines = np.cos(angles).astype(ml_dtypes.bfloat16)
    sines = np.sin(angles[:, 1:half_modes]).astype(ml_dtypes.bfloat16)
    return np.concatenate([cosines, sines], axis=1)


def pick(flag, yes, no):
    return jnp.where(jnp.full(yes.shape, flag, jnp.int32) > 0, yes, no)


def gather_rows(field_ref, col_ref):
    rows, columns = field_ref.shape
    obs = col_ref.shape[1]

    def block(i, seen):
        top = pl.multiple_of(i * 8, 8)
        field = field_ref[pl.ds(top, 8), :]
        cols = col_ref[pl.ds(top, 8), :]
        x_index = lax.broadcasted_iota(jnp.int32, (8, columns), 1)
        lane = lax.broadcasted_iota(jnp.int32, (8, 128), 1)
        found = jnp.zeros((8, 128), jnp.float32)
        for j in range(obs):
            hit = jnp.where(x_index == cols[:, j : j + 1], field, 0.0)
            found = jnp.where(lane == j, jnp.sum(hit, axis=1, keepdims=True), found)
        seen[pl.ds(top, 8), :] = found

    return block


def kernel(
    ns,
    npart,
    norm_factor,
    stream_ref,
    depth_ref,
    col_ref,
    val_ref,
    wgt_ref,
    lw_ref,
    target_ref,
    spec_ref,
    noise_ref,
    sel_ref,
    x_hbm,
    xt_hbm,
    yt_hbm,
    ye_hbm,
    out_ref,
    misfit_ref,
    x_tab,
    xt_tab,
    yt_tab,
    ye_tab,
    tab_sem,
    seen_ref,
    zsend,
    zrecv,
    zs_sem,
    zr_sem,
    noise_a,
    noise_mid,
    noise_b,
    ns_sem,
    nr_sem,
    buf_a,
    mid,
    buf_b,
    as_sem,
    ar_sem,
    bs_sem,
    br_sem,
    dext,
    ds_sem,
    dr_sem,
    w_ref,
    grad,
    send1,
    recv1,
    s1_sem,
    r1_sem,
    st_ref,
    send2,
    recv2,
    s2_sem,
    r2_sem,
    aux_send,
    aux_recv,
    xs_sem,
    xr_sem,
    lhs,
    d_ref,
    d2_ref,
    fin_send,
    fin_recv,
    fs_sem,
    fr_sem,
):
    rows, columns = stream_ref.shape
    obs = col_ref.shape[1]
    kl, n_modes = spec_ref.shape
    ext = rows + 2 * HALO
    me = lax.axis_index("space")
    mp = lax.axis_index("particle")
    p1 = mp + 1 - 2 * (mp % 2)
    p2 = mp + 2 - 4 * ((mp // 2) % 2)
    p3 = p1 + 2 - 4 * ((p1 // 2) % 2)
    above = (me + ns - 1) % ns
    below = (me + 1) % ns
    t0 = sel_ref[0, mp]
    t1 = sel_ref[1, mp]
    t0_far = sel_ref[0, p2]

    loads = []
    for i, (src, dst) in enumerate(((x_hbm, x_tab), (yt_hbm, yt_tab), (ye_hbm, ye_tab), (xt_hbm, xt_tab))):
        copy = pltpu.make_async_copy(src, dst, tab_sem.at[i])
        copy.start()
        loads.append(copy)

    barrier = pltpu.get_barrier_semaphore()
    for off in range(1, ns):
        pl.semaphore_signal(barrier, inc=1, device_id={"particle": mp, "space": (me + off) % ns}, device_id_type=MESH)
    for other in (p1, p2, p3):
        pl.semaphore_signal(barrier, inc=1, device_id={"particle": other, "space": me}, device_id_type=MESH)

    own_block = gather_rows(stream_ref, col_ref)

    @pl.loop(0, rows // 8)
    def _(i):
        own_block(i, seen_ref)

    wide = jnp.concatenate([seen_ref[...], jnp.zeros((128 - rows, 128), jnp.float32)], axis=0)
    zsend[0:obs, :] = wide.T[0:obs, :]
    zsend[obs : obs + 8, :] = jnp.full((8, 128), lw_ref[0], jnp.float32)

    pl.semaphore_wait(barrier, ns - 1 + 3)

    def send(src, dst, s_sem, r_sem, particle, space):
        copy = pltpu.make_async_remote_copy(
            src_ref=src,
            dst_ref=dst,
            send_sem=s_sem,
            recv_sem=r_sem,
            device_id={"particle": particle, "space": space},
            device_id_type=MESH,
        )
        copy.start()
        return copy

    z_copies = [
        send(zsend, zrecv.at[i], zs_sem.at[i], zr_sem.at[i], other, me) for i, other in enumerate((p1, p2, p3))
    ]
    na_copy = send(noise_ref, noise_a, ns_sem.at[0], nr_sem.at[0], p1, me)
    step_rows = rows // PIECES
    part = [pl.ds(i * step_rows, step_rows) for i in range(PIECES)]
    a_copies = [
        send(stream_ref.at[part[i]], buf_a.at[part[i]], as_sem.at[i], ar_sem.at[i], p1, me) for i in range(PIECES)
    ]
    d_copies = [
        send(depth_ref.at[pl.ds(rows - HALO, HALO)], dext.at[pl.ds(0, HALO)], ds_sem.at[0], dr_sem.at[0], mp, below),
        send(depth_ref.at[pl.ds(0, HALO)], dext.at[pl.ds(HALO + rows, HALO)], ds_sem.at[1], dr_sem.at[1], mp, above),
    ]
    spec_t = spec_ref[...].T

    for copy in z_copies:
        copy.wait_recv()
    near = pick(t0, zrecv[0], zsend[...])
    far = pick(t0_far, zrecv[2], zrecv[1])
    chosen = pick(t1, far, near)
    back = jnp.concatenate([chosen, jnp.zeros((128 - obs - 8, 128), jnp.float32)], axis=0).T
    seen = back[0:rows, 0:obs]
    log_weight = back[0:1, obs : obs + 1]
    miss = val_ref[...] - seen
    weighted_miss = wgt_ref[...] * miss
    misfit_part = 0.5 * jnp.sum(weighted_miss * miss, keepdims=True)
    seen_ref[...] = back[0:rows, :]

    @pl.loop(0, rows // 16)
    def _(i):
        top = pl.multiple_of(i * 16, 16)
        cols = col_ref[pl.ds(top, 16), :]
        values = wgt_ref[pl.ds(top, 16), :] * (val_ref[pl.ds(top, 16), :] - seen_ref[pl.ds(top, 16), 0:obs])
        x_index = lax.broadcasted_iota(jnp.int32, (16, columns), 1)
        total = jnp.zeros((16, columns), jnp.float32)
        for j in range(obs):
            total = total + jnp.where(x_index == cols[:, j : j + 1], values[:, j : j + 1], 0.0)
        grad[pl.ds(top, 16), :] = total.astype(jnp.bfloat16)

    loads[0].wait()
    row_modes = jnp.dot(grad[...], x_tab[...], preferred_element_type=jnp.float32)
    for j in range(ns):
        send1[j] = row_modes[:, j * kl : (j + 1) * kl].astype(jnp.bfloat16)
    mine = pl.ds(pl.multiple_of(me * rows, rows), rows)
    copies1 = []
    for off in range(1, ns):
        peer = (me + off) % ns
        copies1.append(send(send1.at[peer], recv1.at[mine], s1_sem.at[off], r1_sem.at[off], mp, peer))
    recv1[mine, :] = send1[me]

    def relay(i):
        a_copies[i].wait_recv()
        mid[part[i], :] = pick(t0, buf_a[part[i], :], stream_ref[part[i], :])
        return send(mid.at[part[i]], buf_b.at[part[i]], bs_sem.at[i], br_sem.at[i], p2, me)

    na_copy.wait_recv()
    noise_mid[...] = pick(t0, noise_a[...].astype(jnp.float32), noise_ref[...].astype(jnp.float32)).astype(jnp.bfloat16)
    nb_copy = send(noise_mid, noise_b, ns_sem.at[1], nr_sem.at[1], p2, me)
    b_copies = [relay(0)]
    shape_gain = jnp.sqrt(norm_factor * spec_ref[...])

    for copy in copies1:
        copy.wait_recv()
    loads[1].wait()
    coef = jnp.dot(yt_tab[...], recv1[...], preferred_element_type=jnp.float32)
    weighted = coef * (norm_factor * spec_t)
    energy_part = jnp.sum(coef * weighted, keepdims=True)
    st_ref[:, 0:kl] = weighted
    nb_copy.wait_recv()
    noise = pick(t1, noise_b[...].astype(jnp.float32), noise_mid[...].astype(jnp.float32))
    st_ref[:, kl : 2 * kl] = (shape_gain * noise).T
    line = lax.broadcasted_iota(jnp.int32, (8, 128), 0)
    aux_send[...] = jnp.where(line == 0, energy_part, jnp.where(line == 1, misfit_part, 0.0))
    loads[2].wait()
    send2[...] = jnp.dot(
        ye_tab[...], st_ref[...].astype(jnp.bfloat16), preferred_element_type=jnp.float32
    ).astype(jnp.bfloat16)
    copies2 = []
    for off in range(1, ns):
        peer = (me + off) % ns
        block = pl.ds(pl.multiple_of(peer * ext, 16), ext)
        copies2.append(send(send2.at[block], recv2.at[me], s2_sem.at[off], r2_sem.at[off], mp, peer))
        copies2.append(send(aux_send, aux_recv.at[me], xs_sem.at[off], xr_sem.at[off], mp, peer))
    recv2[me] = send2[pl.ds(pl.multiple_of(me * ext, 16), ext), :]
    aux_recv[me] = aux_send[...]

    for i in range(1, PIECES):
        b_copies.append(relay(i))

    for copy in d_copies:
        copy.wait_recv()
    dext[HALO : HALO + rows, :] = depth_ref[...]
    grid_row = lax.broadcasted_iota(jnp.int32, (ext, columns), 0) + (me * rows - HALO)
    inside = (grid_row >= 0) & (grid_row < ns * rows)
    w_ref[...] = jnp.where(inside, RELAX_RATE / (4.0 + STRETCH / dext[...]), 0.0)

    for copy in copies2:
        copy.wait_recv()
    for j in range(ns):
        block = recv2[j].astype(jnp.float32)
        lhs[0:ext, j * kl : (j + 1) * kl] = block[:, 0:kl]
        lhs[ext : 2 * ext, j * kl : (j + 1) * kl] = block[:, kl : 2 * kl]
    totals = aux_recv[0]
    for j in range(1, ns):
        totals = totals + aux_recv[j]
    energy = totals[0:1, 0:1]
    misfit = totals[1:2, 0:1]
    step_size = (misfit + log_weight - target_ref[0]) / (energy + 1.0)
    loads[3].wait()
    left = lhs[...].astype(jnp.bfloat16)
    width = columns // 4

    @pl.loop(0, 4)
    def _(i):
        cols = pl.ds(pl.multiple_of(i * width, width), width)
        pulled = jnp.dot(left, xt_tab[:, cols], preferred_element_type=jnp.float32)
        d_ref[:, cols] = step_size * pulled[0:ext] + NOISE_AMP * pulled[ext : 2 * ext]

    def neighbours(field):
        return (
            pltpu.roll(field, 1, 0)
            + pltpu.roll(field, ext - 1, 0)
            + pltpu.roll(field, 1, 1)
            + pltpu.roll(field, columns - 1, 1)
        )

    first = d_ref[...]
    w = w_ref[...]
    once = (1.0 - RELAX_RATE) * first + w * (neighbours(first) - first)
    twice = (1.0 - RELAX_RATE) * once + w * (neighbours(once) - first)
    d2_ref[...] = twice[HALO : HALO + rows, :]

    last_block = gather_rows(d2_ref, col_ref)
    stash = seen_ref[:, 0:obs]

    @pl.loop(0, rows // 8)
    def _(i):
        last_block(i, seen_ref)

    final_miss = val_ref[...] - (stash + seen_ref[:, 0:obs])
    final_part = 0.5 * jnp.sum(wgt_ref[...] * final_miss * final_miss, keepdims=True)
    fin_send[...] = jnp.broadcast_to(final_part, (8, 128))
    copies3 = []
    for off in range(1, ns):
        peer = (me + off) % ns
        copies3.append(send(fin_send, fin_recv.at[me], fs_sem.at[off], fr_sem.at[off], mp, peer))
    fin_recv[me] = fin_send[...]

    for i in range(PIECES):
        b_copies[i].wait_recv()
        out_ref[part[i], :] = pick(t1, buf_b[part[i], :], mid[part[i], :]) + d2_ref[part[i], :]

    for copy in copies3:
        copy.wait_recv()
    final = fin_recv[0]
    for j in range(1, ns):
        final = final + fin_recv[j]
    misfit_ref[...] = final

    for copy in z_copies + [na_copy, nb_copy] + a_copies + b_copies + d_copies + copies1 + copies2 + copies3:
        copy.wait_send()


def per_device(
    ns,
    npart,
    stream,
    depth_field,
    obs_col,
    obs_val,
    obs_weight,
    log_weight,
    target,
    spectrum,
    noise_coef,
    selection,
):
    _, rows, columns = stream.shape
    kl, n_modes = spectrum.shape
    obs = obs_col.shape[1]
    total_rows = rows * ns
    ext = rows + 2 * HALO
    x_np = tables(columns, n_modes // 2)
    y_np = tables(total_rows, n_modes // 2)
    padded = np.pad(y_np, ((HALO, HALO), (0, 0)))
    ye_np = np.concatenate([padded[j * rows : j * rows + ext] for j in range(ns)], axis=0)
    f32, bf16 = jnp.float32, jnp.bfloat16
    vmem = pl.BlockSpec(memory_space=pltpu.VMEM)
    smem = pl.BlockSpec(memory_space=pltpu.SMEM)
    hbm = pl.BlockSpec(memory_space=pl.ANY)
    dma = pltpu.SemaphoreType.DMA
    analysis, misfit = pl.pallas_call(
        functools.partial(kernel, ns, npart, 4.0 / (columns * total_rows)),
        out_shape=(jax.ShapeDtypeStruct((rows, columns), f32), jax.ShapeDtypeStruct((8, 128), f32)),
        in_specs=[vmem] * 5 + [smem, smem, vmem, vmem, smem] + [hbm] * 4,
        out_specs=(vmem, vmem),
        scratch_shapes=[
            pltpu.VMEM((columns, n_modes), bf16),
            pltpu.VMEM((n_modes, columns), bf16),
            pltpu.VMEM((n_modes, total_rows), bf16),
            pltpu.VMEM((ns * ext, n_modes), bf16),
            dma((4,)),
            pltpu.VMEM((rows, 128), f32),
            pltpu.VMEM((obs + 8, 128), f32),
            pltpu.VMEM((3, obs + 8, 128), f32),
            dma((3,)),
            dma((3,)),
            pltpu.VMEM((kl, n_modes), bf16),
            pltpu.VMEM((kl, n_modes), bf16),
            pltpu.VMEM((kl, n_modes), bf16),
            dma((2,)),
            dma((2,)),
            pltpu.VMEM((rows, columns), f32),
            pltpu.VMEM((rows, columns), f32),
            pltpu.VMEM((rows, columns), f32),
            dma((PIECES,)),
            dma((PIECES,)),
            dma((PIECES,)),
            dma((PIECES,)),
            pltpu.VMEM((ext, columns), f32),
            dma((2,)),
            dma((2,)),
            pltpu.VMEM((ext, columns), f32),
            pltpu.VMEM((rows, columns), bf16),
            pltpu.VMEM((ns, rows, kl), bf16),
            pltpu.VMEM((total_rows, kl), bf16),
            dma((ns,)),
            dma((ns,)),
            pltpu.VMEM((n_modes, 2 * kl), f32),
            pltpu.VMEM((ns * ext, 2 * kl), bf16),
            pltpu.VMEM((ns, ext, 2 * kl), bf16),
            dma((ns,)),
            dma((ns,)),
            pltpu.VMEM((8, 128), f32),
            pltpu.VMEM((ns, 8, 128), f32),
            dma((ns,)),
            dma((ns,)),
            pltpu.VMEM((2 * ext, n_modes), f32),
            pltpu.VMEM((ext, columns), f32),
            pltpu.VMEM((rows, columns), f32),
            pltpu.VMEM((8, 128), f32),
            pltpu.VMEM((ns, 8, 128), f32),
            dma((ns,)),
            dma((ns,)),
        ],
        compiler_params=pltpu.CompilerParams(
            collective_id=0, has_side_effects=True, vmem_limit_bytes=48 * 1024 * 1024
        ),
        cost_estimate=pl.CostEstimate(flops=10**9, bytes_accessed=8 * 10**6, transcendentals=0),
    )(
        stream[0],
        depth_field,
        obs_col,
        obs_val,
        obs_weight,
        log_weight,
        target,
        spectrum,
        noise_coef[0],
        selection,
        jnp.asarray(x_np),
        jnp.asarray(np.ascontiguousarray(x_np.T)),
        jnp.asarray(np.ascontiguousarray(y_np.T)),
        jnp.asarray(ye_np),
    )
    return analysis[None], misfit[0, :1]


def solution(mesh):
    return jax.shard_map(
        functools.partial(per_device, mesh.shape["space"], mesh.shape["particle"]),
        mesh=mesh,
        in_specs=(
            P("particle", "space", None),
            P("space", None),
            P("space", None),
            P("space", None),
            P("space", None),
            P("particle"),
            P(),
            P("space", None),
            P("particle", "space", None),
            P(),
        ),
        out_specs=(P("particle", "space", None), P("particle")),
        check_vma=False,
    )
```

```python
import functools
import math

import jax
import jax.numpy as jnp
import ml_dtypes
import numpy as np
from jax import lax
from jax.experimental import pallas as pl
from jax.experimental.pallas import tpu as pltpu
from jax.sharding import PartitionSpec as P

STRETCH = 0.05
RELAX_RATE = 0.8
NOISE_AMP = 0.3
HALO = 8
PIECES = 4
MESH = pl.DeviceIdType.MESH


def tables(extent, half_modes):
    cell_index = np.arange(extent, dtype=np.int32)[:, None]
    frequency = np.arange(half_modes + 1, dtype=np.int32)[None, :]
    angles = (cell_index * frequency % extent).astype(np.float32) * np.float32(2.0 * math.pi / extent)
    cosines = np.cos(angles).astype(ml_dtypes.bfloat16)
    sines = np.sin(angles[:, 1:half_modes]).astype(ml_dtypes.bfloat16)
    return np.concatenate([cosines, sines], axis=1)


def pick(flag, yes, no):
    return jnp.where(jnp.broadcast_to(flag, yes.shape) > 0, yes, no)


def gather_rows(field_ref, col_ref, obs):
    rows, columns = field_ref.shape

    def block(i, seen):
        top = pl.multiple_of(i * 8, 8)
        field = field_ref[pl.ds(top, 8), :]
        cols = col_ref[pl.ds(top, 8), :]
        x_index = lax.broadcasted_iota(jnp.int32, (8, columns), 1).astype(jnp.float32)
        lane = lax.broadcasted_iota(jnp.int32, (8, 128), 1)
        found = jnp.zeros((8, 128), jnp.float32)
        for j in range(obs):
            hit = jnp.where(x_index == cols[:, j : j + 1], field, 0.0)
            found = jnp.where(lane == j, jnp.sum(hit, axis=1, keepdims=True), found)
        seen[pl.ds(top, 8), :] = found

    return block


def kernel(
    ns,
    npart,
    norm_factor,
    stream_hbm,
    depth_hbm,
    col_hbm,
    val_hbm,
    wgt_hbm,
    lw_hbm,
    target_hbm,
    spec_hbm,
    noise_hbm,
    sel_hbm,
    x_hbm,
    xt_hbm,
    yt_hbm,
    ye_hbm,
    out_ref,
    misfit_ref,
    x_tab,
    xt_tab,
    yt_tab,
    ye_tab,
    stream_ref,
    depth_ref,
    obs_ref,
    val_ref,
    wgt_ref,
    lw_ref,
    target_ref,
    spec_ref,
    noise_ref,
    sel_ref,
    col_ref,
    tab_sem,
    seen_ref,
    zsend,
    zrecv,
    zs_sem,
    zr_sem,
    noise_a,
    noise_mid,
    noise_b,
    ns_sem,
    nr_sem,
    buf_a,
    mid,
    buf_b,
    as_sem,
    ar_sem,
    bs_sem,
    br_sem,
    dext,
    ds_sem,
    dr_sem,
    w_ref,
    grad,
    send1,
    recv1,
    s1_sem,
    r1_sem,
    st_ref,
    send2,
    recv2,
    s2_sem,
    r2_sem,
    aux_send,
    aux_recv,
    xs_sem,
    xr_sem,
    lhs,
    d_ref,
    d2_ref,
    fin_send,
    fin_recv,
    fs_sem,
    fr_sem,
):
    rows, columns = stream_ref.shape
    obs = obs_ref.shape[0]
    kl, n_modes = spec_ref.shape
    ext = rows + 2 * HALO
    me = lax.axis_index("space")
    mp = lax.axis_index("particle")
    p1 = mp + 1 - 2 * (mp % 2)
    p2 = mp + 2 - 4 * ((mp // 2) % 2)
    p3 = p1 + 2 - 4 * ((p1 // 2) % 2)
    above = (me + ns - 1) % ns
    below = (me + 1) % ns

    loads = []
    for src, dst in (
        (stream_hbm, stream_ref),
        (col_hbm, obs_ref),
        (val_hbm, val_ref),
        (wgt_hbm, wgt_ref),
        (lw_hbm, lw_ref),
        (sel_hbm, sel_ref),
        (target_hbm, target_ref),
        (x_hbm, x_tab),
        (noise_hbm, noise_ref),
        (spec_hbm, spec_ref),
        (depth_hbm, depth_ref),
        (yt_hbm, yt_tab),
        (ye_hbm, ye_tab),
        (xt_hbm, xt_tab),
    ):
        copy = pltpu.make_async_copy(src, dst, tab_sem.at[len(loads)])
        copy.start()
        loads.append(copy)
    x_load, noise_load, spec_load, depth_load, yt_load, ye_load, xt_load = loads[7:]

    barrier = pltpu.get_barrier_semaphore()
    for off in range(1, ns):
        pl.semaphore_signal(barrier, inc=1, device_id={"particle": mp, "space": (me + off) % ns}, device_id_type=MESH)
    for other in (p1, p2, p3):
        pl.semaphore_signal(barrier, inc=1, device_id={"particle": other, "space": me}, device_id_type=MESH)

    for copy in loads[1:7]:
        copy.wait()
    columns_t = obs_ref[...].astype(jnp.float32)
    col_ref[...] = jnp.concatenate([columns_t, jnp.zeros((128 - obs, rows), jnp.float32)], axis=0).T
    lane_p = lax.broadcasted_iota(jnp.int32, (1, npart), 1)

    def flag(section, slot):
        return jnp.sum(jnp.where(lane_p == slot, sel_ref[section : section + 1, :], 0), axis=1, keepdims=True)

    t0 = flag(0, mp)
    t1 = flag(1, mp)
    t0_far = flag(0, p2)
    loads[0].wait()
    own_block = gather_rows(stream_ref, col_ref, obs)

    @pl.loop(0, rows // 8)
    def _(i):
        own_block(i, seen_ref)

    wide = jnp.concatenate([seen_ref[...], jnp.zeros((128 - rows, 128), jnp.float32)], axis=0)
    zsend[0:obs, :] = wide.T[0:obs, :]
    zsend[obs : obs + 8, :] = jnp.broadcast_to(lw_ref[...], (8, 128))

    pl.semaphore_wait(barrier, ns - 1 + 3)

    def send(src, dst, s_sem, r_sem, particle, space):
        copy = pltpu.make_async_remote_copy(
            src_ref=src,
            dst_ref=dst,
            send_sem=s_sem,
            recv_sem=r_sem,
            device_id={"particle": particle, "space": space},
            device_id_type=MESH,
        )
        copy.start()
        return copy

    z_copies = [
        send(zsend, zrecv.at[i], zs_sem.at[i], zr_sem.at[i], other, me) for i, other in enumerate((p1, p2, p3))
    ]
    na_copy = send(noise_hbm, noise_a, ns_sem.at[0], nr_sem.at[0], p1, me)
    step_rows = rows // PIECES
    part = [pl.ds(i * step_rows, step_rows) for i in range(PIECES)]
    a_copies = [
        send(stream_ref.at[part[i]], buf_a.at[part[i]], as_sem.at[i], ar_sem.at[i], p1, me) for i in range(PIECES)
    ]
    d_copies = [
        send(depth_hbm.at[pl.ds(rows - HALO, HALO)], dext.at[pl.ds(0, HALO)], ds_sem.at[0], dr_sem.at[0], mp, below),
        send(depth_hbm.at[pl.ds(0, HALO)], dext.at[pl.ds(HALO + rows, HALO)], ds_sem.at[1], dr_sem.at[1], mp, above),
    ]
    spec_load.wait()
    spec_t = spec_ref[...].T

    for copy in z_copies:
        copy.wait_recv()
    near = pick(t0, zrecv[0], zsend[...])
    far = pick(t0_far, zrecv[2], zrecv[1])
    chosen = pick(t1, far, near)
    seen = chosen[0:obs, 0:rows]
    log_weight = chosen[obs : obs + 1, 0:1]
    miss = val_ref[...] - seen
    weighted_miss = wgt_ref[...] * miss
    misfit_part = 0.5 * jnp.sum(weighted_miss * miss, keepdims=True)
    seen_ref[...] = jnp.concatenate([weighted_miss, jnp.zeros((128 - obs, rows), jnp.float32)], axis=0).T

    @pl.loop(0, rows // 16)
    def _(i):
        top = pl.multiple_of(i * 16, 16)
        cols = col_ref[pl.ds(top, 16), :]
        values = seen_ref[pl.ds(top, 16), :]
        x_index = lax.broadcasted_iota(jnp.int32, (16, columns), 1).astype(jnp.float32)
        total = jnp.zeros((16, columns), jnp.float32)
        for j in range(obs):
            total = total + jnp.where(x_index == cols[:, j : j + 1], values[:, j : j + 1], 0.0)
        grad[pl.ds(top, 16), :] = total.astype(jnp.bfloat16)

    x_load.wait()
    row_modes = jnp.dot(grad[...], x_tab[...], preferred_element_type=jnp.float32)
    for j in range(ns):
        send1[j] = row_modes[:, j * kl : (j + 1) * kl].astype(jnp.bfloat16)
    mine = pl.ds(pl.multiple_of(me * rows, rows), rows)
    copies1 = []
    for off in range(1, ns):
        peer = (me + off) % ns
        copies1.append(send(send1.at[peer], recv1.at[mine], s1_sem.at[off], r1_sem.at[off], mp, peer))
    recv1[mine, :] = send1[me]

    def relay(i):
        a_copies[i].wait_recv()
        mid[part[i], :] = pick(t0, buf_a[part[i], :], stream_ref[part[i], :])
        return send(mid.at[part[i]], buf_b.at[part[i]], bs_sem.at[i], br_sem.at[i], p2, me)

    na_copy.wait_recv()
    noise_load.wait()
    noise_mid[...] = pick(t0, noise_a[...].astype(jnp.float32), noise_ref[...].astype(jnp.float32)).astype(jnp.bfloat16)
    nb_copy = send(noise_mid, noise_b, ns_sem.at[1], nr_sem.at[1], p2, me)
    b_copies = [relay(0)]
    shape_gain = jnp.sqrt(norm_factor * spec_ref[...])

    for copy in copies1:
        copy.wait_recv()
    yt_load.wait()
    coef = jnp.dot(yt_tab[...], recv1[...], preferred_element_type=jnp.float32)
    weighted = coef * (norm_factor * spec_t)
    energy_part = jnp.sum(coef * weighted, keepdims=True)
    st_ref[:, 0:kl] = weighted
    nb_copy.wait_recv()
    noise = pick(t1, noise_b[...].astype(jnp.float32), noise_mid[...].astype(jnp.float32))
    st_ref[:, kl : 2 * kl] = (shape_gain * noise).T
    line = lax.broadcasted_iota(jnp.int32, (8, 128), 0)
    aux_send[...] = jnp.where(line == 0, energy_part, jnp.where(line == 1, misfit_part, 0.0))
    ye_load.wait()
    send2[...] = jnp.dot(
        ye_tab[...], st_ref[...].astype(jnp.bfloat16), preferred_element_type=jnp.float32
    ).astype(jnp.bfloat16)
    copies2 = []
    for off in range(1, ns):
        peer = (me + off) % ns
        block = pl.ds(pl.multiple_of(peer * ext, 16), ext)
        copies2.append(send(send2.at[block], recv2.at[me], s2_sem.at[off], r2_sem.at[off], mp, peer))
        copies2.append(send(aux_send, aux_recv.at[me], xs_sem.at[off], xr_sem.at[off], mp, peer))
    recv2[me] = send2[pl.ds(pl.multiple_of(me * ext, 16), ext), :]
    aux_recv[me] = aux_send[...]

    for i in range(1, PIECES):
        b_copies.append(relay(i))

    for copy in d_copies:
        copy.wait_recv()
    depth_load.wait()
    dext[HALO : HALO + rows, :] = depth_ref[...]
    grid_row = lax.broadcasted_iota(jnp.int32, (ext, columns), 0) + (me * rows - HALO)
    inside = (grid_row >= 0) & (grid_row < ns * rows)
    w_ref[...] = jnp.where(inside, RELAX_RATE / (4.0 + STRETCH / dext[...]), 0.0)

    for copy in copies2:
        copy.wait_recv()
    for j in range(ns):
        block = recv2[j].astype(jnp.float32)
        lhs[0:ext, j * kl : (j + 1) * kl] = block[:, 0:kl]
        lhs[ext : 2 * ext, j * kl : (j + 1) * kl] = block[:, kl : 2 * kl]
    totals = aux_recv[0]
    for j in range(1, ns):
        totals = totals + aux_recv[j]
    energy = totals[0:1, 0:1]
    misfit = totals[1:2, 0:1]
    step_size = (misfit + log_weight - target_ref[...]) / (energy + 1.0)
    xt_load.wait()
    left = lhs[...].astype(jnp.bfloat16)
    width = columns // 4

    @pl.loop(0, 4)
    def _(i):
        cols = pl.ds(pl.multiple_of(i * width, width), width)
        pulled = jnp.dot(left, xt_tab[:, cols], preferred_element_type=jnp.float32)
        d_ref[:, cols] = step_size * pulled[0:ext] + NOISE_AMP * pulled[ext : 2 * ext]

    def neighbours(field):
        return (
            pltpu.roll(field, 1, 0)
            + pltpu.roll(field, ext - 1, 0)
            + pltpu.roll(field, 1, 1)
            + pltpu.roll(field, columns - 1, 1)
        )

    first = d_ref[...]
    w = w_ref[...]
    once = (1.0 - RELAX_RATE) * first + w * (neighbours(first) - first)
    twice = (1.0 - RELAX_RATE) * once + w * (neighbours(once) - first)
    d2_ref[...] = twice[HALO : HALO + rows, :]

    last_block = gather_rows(d2_ref, col_ref, obs)

    @pl.loop(0, rows // 8)
    def _(i):
        last_block(i, seen_ref)

    moved = jnp.concatenate([seen_ref[...], jnp.zeros((128 - rows, 128), jnp.float32)], axis=0).T[0:obs, 0:rows]
    final_miss = val_ref[...] - (seen + moved)
    final_part = 0.5 * jnp.sum(wgt_ref[...] * final_miss * final_miss, keepdims=True)
    fin_send[...] = jnp.broadcast_to(final_part, (8, 128))
    copies3 = []
    for off in range(1, ns):
        peer = (me + off) % ns
        copies3.append(send(fin_send, fin_recv.at[me], fs_sem.at[off], fr_sem.at[off], mp, peer))
    fin_recv[me] = fin_send[...]

    for i in range(PIECES):
        b_copies[i].wait_recv()
        out_ref[part[i], :] = pick(t1, buf_b[part[i], :], mid[part[i], :]) + d2_ref[part[i], :]

    for copy in copies3:
        copy.wait_recv()
    final = fin_recv[0]
    for j in range(1, ns):
        final = final + fin_recv[j]
    misfit_ref[...] = final

    for copy in z_copies + [na_copy, nb_copy] + a_copies + b_copies + d_copies + copies1 + copies2 + copies3:
        copy.wait_send()


def per_device(
    ns,
    npart,
    stream,
    depth_field,
    obs_col,
    obs_val,
    obs_weight,
    log_weight,
    target,
    spectrum,
    noise_coef,
    selection,
):
    _, rows, columns = stream.shape
    kl, n_modes = spectrum.shape
    obs = obs_col.shape[1]
    total_rows = rows * ns
    ext = rows + 2 * HALO
    x_np = tables(columns, n_modes // 2)
    y_np = tables(total_rows, n_modes // 2)
    padded = np.pad(y_np, ((HALO, HALO), (0, 0)))
    ye_np = np.concatenate([padded[j * rows : j * rows + ext] for j in range(ns)], axis=0)
    f32, bf16 = jnp.float32, jnp.bfloat16
    vmem = pl.BlockSpec(memory_space=pltpu.VMEM)
    hbm = pl.BlockSpec(memory_space=pl.ANY)
    dma = pltpu.SemaphoreType.DMA
    analysis, misfit = pl.pallas_call(
        functools.partial(kernel, ns, npart, 4.0 / (columns * total_rows)),
        out_shape=(jax.ShapeDtypeStruct((rows, columns), f32), jax.ShapeDtypeStruct((8, 128), f32)),
        in_specs=[hbm] * 14,
        out_specs=(vmem, vmem),
        scratch_shapes=[
            pltpu.VMEM((columns, n_modes), bf16),
            pltpu.VMEM((n_modes, columns), bf16),
            pltpu.VMEM((n_modes, total_rows), bf16),
            pltpu.VMEM((ns * ext, n_modes), bf16),
            pltpu.VMEM((rows, columns), f32),
            pltpu.VMEM((rows, columns), f32),
            pltpu.VMEM((obs, rows), jnp.int32),
            pltpu.VMEM((obs, rows), f32),
            pltpu.VMEM((obs, rows), f32),
            pltpu.VMEM((1, 1), f32),
            pltpu.VMEM((1, 1), f32),
            pltpu.VMEM((kl, n_modes), f32),
            pltpu.VMEM((kl, n_modes), bf16),
            pltpu.VMEM(selection.shape, jnp.int32),
            pltpu.VMEM((rows, 128), f32),
            dma((14,)),
            pltpu.VMEM((rows, 128), f32),
            pltpu.VMEM((obs + 8, 128), f32),
            pltpu.VMEM((3, obs + 8, 128), f32),
            dma((3,)),
            dma((3,)),
            pltpu.VMEM((kl, n_modes), bf16),
            pltpu.VMEM((kl, n_modes), bf16),
            pltpu.VMEM((kl, n_modes), bf16),
            dma((2,)),
            dma((2,)),
            pltpu.VMEM((rows, columns), f32),
            pltpu.VMEM((rows, columns), f32),
            pltpu.VMEM((rows, columns), f32),
            dma((PIECES,)),
            dma((PIECES,)),
            dma((PIECES,)),
            dma((PIECES,)),
            pltpu.VMEM((ext, columns), f32),
            dma((2,)),
            dma((2,)),
            pltpu.VMEM((ext, columns), f32),
            pltpu.VMEM((rows, columns), bf16),
            pltpu.VMEM((ns, rows, kl), bf16),
            pltpu.VMEM((total_rows, kl), bf16),
            dma((ns,)),
            dma((ns,)),
            pltpu.VMEM((n_modes, 2 * kl), f32),
            pltpu.VMEM((ns * ext, 2 * kl), bf16),
            pltpu.VMEM((ns, ext, 2 * kl), bf16),
            dma((ns,)),
            dma((ns,)),
            pltpu.VMEM((8, 128), f32),
            pltpu.VMEM((ns, 8, 128), f32),
            dma((ns,)),
            dma((ns,)),
            pltpu.VMEM((2 * ext, n_modes), f32),
            pltpu.VMEM((ext, columns), f32),
            pltpu.VMEM((rows, columns), f32),
            pltpu.VMEM((8, 128), f32),
            pltpu.VMEM((ns, 8, 128), f32),
            dma((ns,)),
            dma((ns,)),
        ],
        compiler_params=pltpu.CompilerParams(
            collective_id=0, has_side_effects=True, vmem_limit_bytes=60 * 1024 * 1024
        ),
        cost_estimate=pl.CostEstimate(flops=10**9, bytes_accessed=8 * 10**6, transcendentals=0),
    )(
        stream[0],
        depth_field,
        obs_col.T,
        obs_val.T,
        obs_weight.T,
        log_weight.reshape(1, 1),
        target.reshape(1, 1),
        spectrum,
        noise_coef[0],
        selection,
        jnp.asarray(x_np),
        jnp.asarray(np.ascontiguousarray(x_np.T)),
        jnp.asarray(np.ascontiguousarray(y_np.T)),
        jnp.asarray(ye_np),
    )
    return analysis[None], misfit[0, :1]


def solution(mesh):
    return jax.shard_map(
        functools.partial(per_device, mesh.shape["space"], mesh.shape["particle"]),
        mesh=mesh,
        in_specs=(
            P("particle", "space", None),
            P("space", None),
            P("space", None),
            P("space", None),
            P("space", None),
            P("particle"),
            P(),
            P("space", None),
            P("particle", "space", None),
            P(),
        ),
        out_specs=(P("particle", "space", None), P("particle")),
        check_vma=False,
    )
```

```python
import functools
import math

import jax
import jax.numpy as jnp
import ml_dtypes
import numpy as np
from jax import lax
from jax.experimental import pallas as pl
from jax.experimental.pallas import tpu as pltpu
from jax.sharding import PartitionSpec as P

STRETCH = 0.05
RELAX_RATE = 0.8
NOISE_AMP = 0.3
HALO = 8
PIECES = 4
CODE_SCALE = 256.0
CODE_LEAST = 2.0**-126
MESH = pl.DeviceIdType.MESH


def tables(extent, half_modes):
    cell_index = np.arange(extent, dtype=np.int32)[:, None]
    frequency = np.arange(half_modes + 1, dtype=np.int32)[None, :]
    angles = (cell_index * frequency % extent).astype(np.float32) * np.float32(2.0 * math.pi / extent)
    cosines = np.cos(angles).astype(ml_dtypes.bfloat16)
    sines = np.sin(angles[:, 1:half_modes]).astype(ml_dtypes.bfloat16)
    return np.concatenate([cosines, sines], axis=1)


def pick(flag, yes, no):
    return jnp.where(jnp.broadcast_to(flag, yes.shape) > 0, yes, no)


def coded(value):
    scaled = value * CODE_SCALE
    sixth = (scaled * scaled * scaled) * (scaled * scaled * scaled)
    power = sixth * sixth
    return jnp.where(value < 0.0, -power, power).astype(jnp.bfloat16)


def decoded(code):
    size = jnp.exp2(jnp.log2(jnp.maximum(jnp.abs(code), CODE_LEAST)) * (1.0 / 12.0)) * (1.0 / CODE_SCALE)
    return jnp.where(code < 0.0, -size, size)


def gather_rows(field_ref, col_ref, obs):
    rows, columns = field_ref.shape

    def block(i, seen):
        top = pl.multiple_of(i * 8, 8)
        field = field_ref[pl.ds(top, 8), :]
        cols = col_ref[pl.ds(top, 8), :]
        x_index = lax.broadcasted_iota(jnp.int32, (8, columns), 1).astype(jnp.float32)
        lane = lax.broadcasted_iota(jnp.int32, (8, 128), 1)
        found = jnp.zeros((8, 128), jnp.float32)
        for j in range(obs):
            hit = jnp.where(x_index == cols[:, j : j + 1], field, 0.0)
            found = jnp.where(lane == j, jnp.sum(hit, axis=1, keepdims=True), found)
        seen[pl.ds(top, 8), :] = found

    return block


def kernel(
    ns,
    npart,
    norm_factor,
    stream_hbm,
    depth_hbm,
    col_hbm,
    val_hbm,
    wgt_hbm,
    lw_hbm,
    target_hbm,
    spec_hbm,
    noise_hbm,
    sel_hbm,
    x_hbm,
    xt_hbm,
    yt_hbm,
    ye_hbm,
    out_ref,
    misfit_ref,
    x_tab,
    xt_tab,
    yt_tab,
    ye_tab,
    stream_ref,
    depth_ref,
    obs_ref,
    val_ref,
    wgt_ref,
    lw_ref,
    target_ref,
    spec_ref,
    noise_ref,
    sel_ref,
    col_ref,
    tab_sem,
    seen_ref,
    zsend,
    zrecv,
    zs_sem,
    zr_sem,
    noise_a,
    noise_mid,
    noise_b,
    ns_sem,
    nr_sem,
    code,
    buf_a,
    mid,
    buf_b,
    as_sem,
    ar_sem,
    bs_sem,
    br_sem,
    dext,
    ds_sem,
    dr_sem,
    w_ref,
    grad,
    send1,
    recv1,
    s1_sem,
    r1_sem,
    st_ref,
    send2,
    recv2,
    s2_sem,
    r2_sem,
    aux_send,
    aux_recv,
    xs_sem,
    xr_sem,
    lhs,
    d_ref,
    d2_ref,
    fin_send,
    fin_recv,
    fs_sem,
    fr_sem,
):
    rows, columns = stream_ref.shape
    obs = obs_ref.shape[0]
    kl, n_modes = spec_ref.shape
    ext = rows + 2 * HALO
    me = lax.axis_index("space")
    mp = lax.axis_index("particle")
    p1 = mp + 1 - 2 * (mp % 2)
    p2 = mp + 2 - 4 * ((mp // 2) % 2)
    p3 = p1 + 2 - 4 * ((p1 // 2) % 2)
    above = (me + ns - 1) % ns
    below = (me + 1) % ns

    loads = []
    for src, dst in (
        (stream_hbm, stream_ref),
        (col_hbm, obs_ref),
        (val_hbm, val_ref),
        (wgt_hbm, wgt_ref),
        (lw_hbm, lw_ref),
        (sel_hbm, sel_ref),
        (target_hbm, target_ref),
        (x_hbm, x_tab),
        (noise_hbm, noise_ref),
        (spec_hbm, spec_ref),
        (depth_hbm, depth_ref),
        (yt_hbm, yt_tab),
        (ye_hbm, ye_tab),
        (xt_hbm, xt_tab),
    ):
        copy = pltpu.make_async_copy(src, dst, tab_sem.at[len(loads)])
        copy.start()
        loads.append(copy)
    x_load, noise_load, spec_load, depth_load, yt_load, ye_load, xt_load = loads[7:]

    barrier = pltpu.get_barrier_semaphore()
    for off in range(1, ns):
        pl.semaphore_signal(barrier, inc=1, device_id={"particle": mp, "space": (me + off) % ns}, device_id_type=MESH)
    for other in (p1, p2, p3):
        pl.semaphore_signal(barrier, inc=1, device_id={"particle": other, "space": me}, device_id_type=MESH)

    for copy in loads[1:7]:
        copy.wait()
    columns_t = obs_ref[...].astype(jnp.float32)
    col_ref[...] = jnp.concatenate([columns_t, jnp.zeros((128 - obs, rows), jnp.float32)], axis=0).T
    lane_p = lax.broadcasted_iota(jnp.int32, (1, npart), 1)

    def flag(section, slot):
        return jnp.sum(jnp.where(lane_p == slot, sel_ref[section : section + 1, :], 0), axis=1, keepdims=True)

    t0 = flag(0, mp)
    t1 = flag(1, mp)
    t0_far = flag(0, p2)
    loads[0].wait()
    own_block = gather_rows(stream_ref, col_ref, obs)

    @pl.loop(0, rows // 8)
    def _(i):
        own_block(i, seen_ref)

    wide = jnp.concatenate([seen_ref[...], jnp.zeros((128 - rows, 128), jnp.float32)], axis=0)
    zsend[0:obs, :] = wide.T[0:obs, :]
    zsend[obs : obs + 8, :] = jnp.broadcast_to(lw_ref[...], (8, 128))

    pl.semaphore_wait(barrier, ns - 1 + 3)

    def send(src, dst, s_sem, r_sem, particle, space):
        copy = pltpu.make_async_remote_copy(
            src_ref=src,
            dst_ref=dst,
            send_sem=s_sem,
            recv_sem=r_sem,
            device_id={"particle": particle, "space": space},
            device_id_type=MESH,
        )
        copy.start()
        return copy

    z_copies = [
        send(zsend, zrecv.at[i], zs_sem.at[i], zr_sem.at[i], other, me) for i, other in enumerate((p1, p2, p3))
    ]
    na_copy = send(noise_hbm, noise_a, ns_sem.at[0], nr_sem.at[0], p1, me)
    step_rows = rows // PIECES
    part = [pl.ds(i * step_rows, step_rows) for i in range(PIECES)]
    code[...] = coded(stream_ref[...])
    a_copies = [
        send(code.at[part[i]], buf_a.at[part[i]], as_sem.at[i], ar_sem.at[i], p1, me) for i in range(PIECES)
    ]
    d_copies = [
        send(depth_hbm.at[pl.ds(rows - HALO, HALO)], dext.at[pl.ds(0, HALO)], ds_sem.at[0], dr_sem.at[0], mp, below),
        send(depth_hbm.at[pl.ds(0, HALO)], dext.at[pl.ds(HALO + rows, HALO)], ds_sem.at[1], dr_sem.at[1], mp, above),
    ]
    spec_load.wait()
    spec_t = spec_ref[...].T

    for copy in z_copies:
        copy.wait_recv()
    near = pick(t0, zrecv[0], zsend[...])
    far = pick(t0_far, zrecv[2], zrecv[1])
    chosen = pick(t1, far, near)
    seen = chosen[0:obs, 0:rows]
    log_weight = chosen[obs : obs + 1, 0:1]
    miss = val_ref[...] - seen
    weighted_miss = wgt_ref[...] * miss
    misfit_part = 0.5 * jnp.sum(weighted_miss * miss, keepdims=True)
    seen_ref[...] = jnp.concatenate([weighted_miss, jnp.zeros((128 - obs, rows), jnp.float32)], axis=0).T

    @pl.loop(0, rows // 16)
    def _(i):
        top = pl.multiple_of(i * 16, 16)
        cols = col_ref[pl.ds(top, 16), :]
        values = seen_ref[pl.ds(top, 16), :]
        x_index = lax.broadcasted_iota(jnp.int32, (16, columns), 1).astype(jnp.float32)
        total = jnp.zeros((16, columns), jnp.float32)
        for j in range(obs):
            total = total + jnp.where(x_index == cols[:, j : j + 1], values[:, j : j + 1], 0.0)
        grad[pl.ds(top, 16), :] = total.astype(jnp.bfloat16)

    x_load.wait()
    row_modes = jnp.dot(grad[...], x_tab[...], preferred_element_type=jnp.float32)
    for j in range(ns):
        send1[j] = row_modes[:, j * kl : (j + 1) * kl].astype(jnp.bfloat16)
    mine = pl.ds(pl.multiple_of(me * rows, rows), rows)
    copies1 = []
    for off in range(1, ns):
        peer = (me + off) % ns
        copies1.append(send(send1.at[peer], recv1.at[mine], s1_sem.at[off], r1_sem.at[off], mp, peer))
    recv1[mine, :] = send1[me]

    def relay(i):
        a_copies[i].wait_recv()
        mid[part[i], :] = pick(
            t0, buf_a[part[i], :].astype(jnp.float32), code[part[i], :].astype(jnp.float32)
        ).astype(jnp.bfloat16)
        return send(mid.at[part[i]], buf_b.at[part[i]], bs_sem.at[i], br_sem.at[i], p2, me)

    na_copy.wait_recv()
    noise_load.wait()
    noise_mid[...] = pick(t0, noise_a[...].astype(jnp.float32), noise_ref[...].astype(jnp.float32)).astype(jnp.bfloat16)
    nb_copy = send(noise_mid, noise_b, ns_sem.at[1], nr_sem.at[1], p2, me)
    b_copies = [relay(0)]
    shape_gain = jnp.sqrt(norm_factor * spec_ref[...])

    for copy in copies1:
        copy.wait_recv()
    yt_load.wait()
    coef = jnp.dot(yt_tab[...], recv1[...], preferred_element_type=jnp.float32)
    weighted = coef * (norm_factor * spec_t)
    energy_part = jnp.sum(coef * weighted, keepdims=True)
    st_ref[:, 0:kl] = weighted
    nb_copy.wait_recv()
    noise = pick(t1, noise_b[...].astype(jnp.float32), noise_mid[...].astype(jnp.float32))
    st_ref[:, kl : 2 * kl] = (shape_gain * noise).T
    line = lax.broadcasted_iota(jnp.int32, (8, 128), 0)
    aux_send[...] = jnp.where(line == 0, energy_part, jnp.where(line == 1, misfit_part, 0.0))
    ye_load.wait()
    send2[...] = jnp.dot(
        ye_tab[...], st_ref[...].astype(jnp.bfloat16), preferred_element_type=jnp.float32
    ).astype(jnp.bfloat16)
    copies2 = []
    for off in range(1, ns):
        peer = (me + off) % ns
        block = pl.ds(pl.multiple_of(peer * ext, 16), ext)
        copies2.append(send(send2.at[block], recv2.at[me], s2_sem.at[off], r2_sem.at[off], mp, peer))
        copies2.append(send(aux_send, aux_recv.at[me], xs_sem.at[off], xr_sem.at[off], mp, peer))
    recv2[me] = send2[pl.ds(pl.multiple_of(me * ext, 16), ext), :]
    aux_recv[me] = aux_send[...]

    for i in range(1, PIECES):
        b_copies.append(relay(i))

    for copy in d_copies:
        copy.wait_recv()
    depth_load.wait()
    dext[HALO : HALO + rows, :] = depth_ref[...]
    grid_row = lax.broadcasted_iota(jnp.int32, (ext, columns), 0) + (me * rows - HALO)
    inside = (grid_row >= 0) & (grid_row < ns * rows)
    w_ref[...] = jnp.where(inside, RELAX_RATE / (4.0 + STRETCH / dext[...]), 0.0)

    for copy in copies2:
        copy.wait_recv()
    for j in range(ns):
        block = recv2[j].astype(jnp.float32)
        lhs[0:ext, j * kl : (j + 1) * kl] = block[:, 0:kl]
        lhs[ext : 2 * ext, j * kl : (j + 1) * kl] = block[:, kl : 2 * kl]
    totals = aux_recv[0]
    for j in range(1, ns):
        totals = totals + aux_recv[j]
    energy = totals[0:1, 0:1]
    misfit = totals[1:2, 0:1]
    step_size = (misfit + log_weight - target_ref[...]) / (energy + 1.0)
    xt_load.wait()
    left = lhs[...].astype(jnp.bfloat16)
    width = columns // 4

    @pl.loop(0, 4)
    def _(i):
        cols = pl.ds(pl.multiple_of(i * width, width), width)
        pulled = jnp.dot(left, xt_tab[:, cols], preferred_element_type=jnp.float32)
        d_ref[:, cols] = step_size * pulled[0:ext] + NOISE_AMP * pulled[ext : 2 * ext]

    def neighbours(field):
        return (
            pltpu.roll(field, 1, 0)
            + pltpu.roll(field, ext - 1, 0)
            + pltpu.roll(field, 1, 1)
            + pltpu.roll(field, columns - 1, 1)
        )

    first = d_ref[...]
    w = w_ref[...]
    once = (1.0 - RELAX_RATE) * first + w * (neighbours(first) - first)
    twice = (1.0 - RELAX_RATE) * once + w * (neighbours(once) - first)
    d2_ref[...] = twice[HALO : HALO + rows, :]

    last_block = gather_rows(d2_ref, col_ref, obs)

    @pl.loop(0, rows // 8)
    def _(i):
        last_block(i, seen_ref)

    moved = jnp.concatenate([seen_ref[...], jnp.zeros((128 - rows, 128), jnp.float32)], axis=0).T[0:obs, 0:rows]
    final_miss = val_ref[...] - (seen + moved)
    final_part = 0.5 * jnp.sum(wgt_ref[...] * final_miss * final_miss, keepdims=True)
    fin_send[...] = jnp.broadcast_to(final_part, (8, 128))
    copies3 = []
    for off in range(1, ns):
        peer = (me + off) % ns
        copies3.append(send(fin_send, fin_recv.at[me], fs_sem.at[off], fr_sem.at[off], mp, peer))
    fin_recv[me] = fin_send[...]

    for i in range(PIECES):
        b_copies[i].wait_recv()
        came = pick(t1, buf_b[part[i], :].astype(jnp.float32), mid[part[i], :].astype(jnp.float32))
        out_ref[part[i], :] = pick(t0 + t1, decoded(came), stream_ref[part[i], :]) + d2_ref[part[i], :]

    for copy in copies3:
        copy.wait_recv()
    final = fin_recv[0]
    for j in range(1, ns):
        final = final + fin_recv[j]
    misfit_ref[...] = final

    for copy in z_copies + [na_copy, nb_copy] + a_copies + b_copies + d_copies + copies1 + copies2 + copies3:
        copy.wait_send()


def per_device(
    ns,
    npart,
    stream,
    depth_field,
    obs_col,
    obs_val,
    obs_weight,
    log_weight,
    target,
    spectrum,
    noise_coef,
    selection,
):
    _, rows, columns = stream.shape
    kl, n_modes = spectrum.shape
    obs = obs_col.shape[1]
    total_rows = rows * ns
    ext = rows + 2 * HALO
    x_np = tables(columns, n_modes // 2)
    y_np = tables(total_rows, n_modes // 2)
    padded = np.pad(y_np, ((HALO, HALO), (0, 0)))
    ye_np = np.concatenate([padded[j * rows : j * rows + ext] for j in range(ns)], axis=0)
    f32, bf16 = jnp.float32, jnp.bfloat16
    vmem = pl.BlockSpec(memory_space=pltpu.VMEM)
    hbm = pl.BlockSpec(memory_space=pl.ANY)
    dma = pltpu.SemaphoreType.DMA
    analysis, misfit = pl.pallas_call(
        functools.partial(kernel, ns, npart, 4.0 / (columns * total_rows)),
        out_shape=(jax.ShapeDtypeStruct((rows, columns), f32), jax.ShapeDtypeStruct((8, 128), f32)),
        in_specs=[hbm] * 14,
        out_specs=(vmem, vmem),
        scratch_shapes=[
            pltpu.VMEM((columns, n_modes), bf16),
            pltpu.VMEM((n_modes, columns), bf16),
            pltpu.VMEM((n_modes, total_rows), bf16),
            pltpu.VMEM((ns * ext, n_modes), bf16),
            pltpu.VMEM((rows, columns), f32),
            pltpu.VMEM((rows, columns), f32),
            pltpu.VMEM((obs, rows), jnp.int32),
            pltpu.VMEM((obs, rows), f32),
            pltpu.VMEM((obs, rows), f32),
            pltpu.VMEM((1, 1), f32),
            pltpu.VMEM((1, 1), f32),
            pltpu.VMEM((kl, n_modes), f32),
            pltpu.VMEM((kl, n_modes), bf16),
            pltpu.VMEM(selection.shape, jnp.int32),
            pltpu.VMEM((rows, 128), f32),
            dma((14,)),
            pltpu.VMEM((rows, 128), f32),
            pltpu.VMEM((obs + 8, 128), f32),
            pltpu.VMEM((3, obs + 8, 128), f32),
            dma((3,)),
            dma((3,)),
            pltpu.VMEM((kl, n_modes), bf16),
            pltpu.VMEM((kl, n_modes), bf16),
            pltpu.VMEM((kl, n_modes), bf16),
            dma((2,)),
            dma((2,)),
            pltpu.VMEM((rows, columns), bf16),
            pltpu.VMEM((rows, columns), bf16),
            pltpu.VMEM((rows, columns), bf16),
            pltpu.VMEM((rows, columns), bf16),
            dma((PIECES,)),
            dma((PIECES,)),
            dma((PIECES,)),
            dma((PIECES,)),
            pltpu.VMEM((ext, columns), f32),
            dma((2,)),
            dma((2,)),
            pltpu.VMEM((ext, columns), f32),
            pltpu.VMEM((rows, columns), bf16),
            pltpu.VMEM((ns, rows, kl), bf16),
            pltpu.VMEM((total_rows, kl), bf16),
            dma((ns,)),
            dma((ns,)),
            pltpu.VMEM((n_modes, 2 * kl), f32),
            pltpu.VMEM((ns * ext, 2 * kl), bf16),
            pltpu.VMEM((ns, ext, 2 * kl), bf16),
            dma((ns,)),
            dma((ns,)),
            pltpu.VMEM((8, 128), f32),
            pltpu.VMEM((ns, 8, 128), f32),
            dma((ns,)),
            dma((ns,)),
            pltpu.VMEM((2 * ext, n_modes), f32),
            pltpu.VMEM((ext, columns), f32),
            pltpu.VMEM((rows, columns), f32),
            pltpu.VMEM((8, 128), f32),
            pltpu.VMEM((ns, 8, 128), f32),
            dma((ns,)),
            dma((ns,)),
        ],
        compiler_params=pltpu.CompilerParams(
            collective_id=0, has_side_effects=True, vmem_limit_bytes=60 * 1024 * 1024
        ),
        cost_estimate=pl.CostEstimate(flops=10**9, bytes_accessed=8 * 10**6, transcendentals=0),
    )(
        stream[0],
        depth_field,
        obs_col.T,
        obs_val.T,
        obs_weight.T,
        log_weight.reshape(1, 1),
        target.reshape(1, 1),
        spectrum,
        noise_coef[0],
        selection,
        jnp.asarray(x_np),
        jnp.asarray(np.ascontiguousarray(x_np.T)),
        jnp.asarray(np.ascontiguousarray(y_np.T)),
        jnp.asarray(ye_np),
    )
    return analysis[None], misfit[0, :1]


def solution(mesh):
    return jax.shard_map(
        functools.partial(per_device, mesh.shape["space"], mesh.shape["particle"]),
        mesh=mesh,
        in_specs=(
            P("particle", "space", None),
            P("space", None),
            P("space", None),
            P("space", None),
            P("space", None),
            P("particle"),
            P(),
            P("space", None),
            P("particle", "space", None),
            P(),
        ),
        out_specs=(P("particle", "space", None), P("particle")),
        check_vma=False,
    )
```
